32 devices in a mesh: row: 4 (over y, x), col: 8 (over z, core).
Axes of the slice: x: 2, y: 2, z: 4, core: 2. Of those that a mesh axis runs over, the one named last changes fastest.
Arguments:
- amplitudes: bfloat16 [10240, 8192], P('row', 'col'), may hold values from -6 to 6
- integrals: bfloat16 [1280, 128, 128], P(('row', 'col')), may hold values from -0.1875 to 0.1875
- tile_ab: int32 [1280], P(('row', 'col')), may hold values from -1 to 19, as said below
- tile_cd: int32 [1280], P(('row', 'col')), may hold values from -1 to 79, as said below
Outputs:
- residual: bfloat16 [10240, 8192], P('row', 'col')
The draws below stay inside these ranges and needn't reach their ends.
Inputs may be any that keep to these rules, and one draw needn't show every extreme that they name: A slot is live where tile_ab >= 0; then tile_cd >= 0 as well. Empty slots have -1 in both. Each device's live slots come before its empty ones. The live (tile_ab, tile_cd) pairs of one row group are distinct. Each row group holds exactly 145 live slots, and one device of each row group has all its 40 slots live. `tile_cd`: see tile_ab.
All inputs are finite; a program needn't handle non-finite values.
Results may differ from the reference program's by a relative error of at most 0.001.
Values may be sent and summed in bfloat16 or wider, within the bound.
A program may use at most 320 MiB of HBM per device.

```python
import jax
import jax.numpy as jnp
from jax import lax

TILE = 128
NV = 80
SLOTS = 40
ROW_TILES = 20
GROUP_SLOTS = 320
NNZR = 145
OCC_ALL = 8192
N_ROW = 4
N_COL = 8


def slot_layout(key):
    candidates = NV // N_ROW * NV
    keys = jax.random.split(key, 3)
    row_keys = jax.random.split(keys[0], N_ROW)
    orders = jax.vmap(lambda one_key: jax.random.permutation(one_key, candidates))(row_keys)
    spread = SLOTS // 8
    middle = SLOTS // 4 + spread
    wobble = jax.random.randint(keys[1], (N_ROW, N_COL - 1), 0, spread + 1)
    others = middle + wobble - jnp.roll(wobble, -1, axis=1)
    busiest = jax.random.randint(keys[2], (N_ROW, 1), 0, N_COL)
    column = jnp.broadcast_to(jnp.arange(N_COL)[None, :], (N_ROW, N_COL))
    lookup = jnp.clip(column - (column > busiest).astype(jnp.int32), 0, N_COL - 2)
    counts = jnp.where(column == busiest, SLOTS, jnp.take_along_axis(others, lookup, axis=1))
    offsets = jnp.cumsum(counts, axis=1) - counts
    slot_number = jnp.arange(SLOTS)
    index = offsets[:, :, None] + slot_number[None, None, :]
    live_mask = slot_number[None, None, :] < counts[:, :, None]
    group_number = jnp.arange(N_ROW)[:, None, None]
    picked = orders[group_number, jnp.clip(index, 0, candidates - 1)]
    ab_index = jnp.where(live_mask, picked // NV, -1).reshape(-1)
    cd_index = jnp.where(live_mask, picked % NV, -1).reshape(-1)
    return (ab_index.astype(jnp.int32), cd_index.astype(jnp.int32))


def draw_tile_ab(key, part):
    return slot_layout(key)[0]


def draw_tile_cd(key, part):
    return slot_layout(key)[1]


def block_levels(own_key, shape, shards, low, largest):
    loudness, own = 1.0, jax.random.fold_in(own_key, 6)
    for dim, parts in shards:
        draws = jnp.exp(jax.random.uniform(jax.random.fold_in(own, dim), (parts,), jnp.float32, low / len(shards), largest / len(shards)))
        loudness = loudness * jnp.repeat(draws, shape[dim] // parts).reshape([-1 if axis == dim else 1 for axis in range(len(shape))])
    return loudness


def normal_values(rng, dims, width, reach, cuts=(), held_as=jnp.bfloat16):
    drawn = width * jax.random.normal(rng, dims, jnp.float32)
    if cuts:
        drawn = drawn * block_levels(rng, dims, cuts, -0.22, 0.18)
    return jnp.clip(drawn, -reach, reach).astype(held_as)


def setup_inputs(seed: int = 0) -> dict:
    key_list = jax.random.split(jax.random.key(seed), 5)
    amplitudes = normal_values(key_list[0], (NV * TILE, OCC_ALL), 1.0, 6.0, ((0, 4), (1, 8)))
    integrals = normal_values(key_list[1], (N_ROW * GROUP_SLOTS, TILE, TILE), (NNZR * TILE // ROW_TILES) ** -0.5, 0.1875, ((0, 32),))
    tile_ab = draw_tile_ab(jax.random.fold_in(key_list[4], 71), 0)
    tile_cd = draw_tile_cd(jax.random.fold_in(key_list[4], 71), 0)
    return {"amplitudes": amplitudes, "integrals": integrals, "tile_ab": tile_ab, "tile_cd": tile_cd}


def reference(amplitudes, integrals, tile_ab, tile_cd):
    row_tiles = NV // N_ROW
    group_slots = N_COL * SLOTS
    group_data = integrals.reshape(N_ROW, group_slots, TILE, TILE)
    group_ab = tile_ab.reshape(N_ROW, group_slots)
    group_cd = tile_cd.reshape(N_ROW, group_slots)

    def one_group(packed):
        tile_data, ab_index, cd_index = packed
        position = jnp.where(ab_index >= 0, ab_index * NV + cd_index, row_tiles * NV).astype(jnp.int32)
        dense_block = jnp.zeros((row_tiles * NV, TILE, TILE), jnp.bfloat16)
        dense_block = dense_block.at[position].add(tile_data, mode="drop")
        matrix = dense_block.reshape(row_tiles, NV, TILE, TILE).transpose(0, 2, 1, 3).reshape(row_tiles * TILE, NV * TILE)
        return jnp.dot(matrix, amplitudes, preferred_element_type=jnp.float32).astype(jnp.bfloat16)

    blocks = lax.map(one_group, (group_data, group_ab, group_cd))
    return blocks.reshape(NV * TILE, amplitudes.shape[1])
```

```python
import jax
import jax.numpy as jnp
from jax import lax
from jax.experimental import pallas as pl
from jax.experimental.pallas import tpu as pltpu
from jax.sharding import PartitionSpec as P

TILE = 128
NV = 80
MESH = pl.DeviceIdType.MESH
CHUNK = 256
GROUP = 5
WIDE = 256


def place_tiles(dense_block, pieces):
    tile_data, ab_code, cd_code = pieces
    ab_index = ab_code.astype(jnp.int32)
    cd_index = cd_code.astype(jnp.int32)
    position = jnp.where(ab_index >= 0, ab_index * NV + cd_index, dense_block.shape[0])
    return dense_block.at[position].add(tile_data, mode="drop")


def plain_body(amplitudes, integrals, tile_ab, tile_cd):
    row_tiles = amplitudes.shape[0] // TILE
    ab_code = tile_ab.astype(jnp.bfloat16)
    cd_code = tile_cd.astype(jnp.bfloat16)
    empty_block = jnp.zeros((row_tiles * NV, TILE, TILE), jnp.bfloat16)
    dense_block = place_tiles(
        empty_block,
        (
            lax.all_gather(integrals, "col", axis=0, tiled=True),
            lax.all_gather(ab_code, "col", axis=0, tiled=True),
            lax.all_gather(cd_code, "col", axis=0, tiled=True),
        ),
    )
    matrix = (
        dense_block.reshape(row_tiles, NV, TILE, TILE)
        .transpose(0, 2, 1, 3)
        .reshape(row_tiles * TILE, NV * TILE)
    )
    result = jnp.dot(
        matrix,
        lax.all_gather(amplitudes, "row", axis=0, tiled=True),
        preferred_element_type=jnp.float32,
    )
    return result.astype(jnp.bfloat16)


def ladder_kernel(
    amp, ints, codes_in, out, a_all, v_all, codes, place, place_s, lhs, acc, stage,
    own_sem, code_send, code_recv, xs, xr, ys, yr, fxs, fxr, fys, fyr,
    up_s, down_s, line_r, sib_s, sib_r, out_sem,
):
    rows, width = amp.shape
    slots = ints.shape[0]
    chunks = rows // CHUNK
    half = chunks // 2
    row_tiles = rows // TILE
    n_col = codes.shape[0]
    n_z = n_col // 2
    empty = n_col * slots

    r = lax.axis_index("row")
    c = lax.axis_index("col")
    x, y = r % 2, r // 2
    xn, yn, dg = r + 1 - 2 * x, r + 2 - 4 * y, 3 - r
    z, core = c // 2, c % 2
    sib = c + 1 - 2 * core

    barrier = pltpu.get_barrier_semaphore()
    for row in (xn, yn):
        pl.semaphore_signal(barrier, inc=1, device_id=(row, c), device_id_type=MESH)
    for d in range(1, n_col):
        pl.semaphore_signal(barrier, inc=1, device_id=(r, (c + d) % n_col), device_id_type=MESH)
    pl.semaphore_wait(barrier, n_col + 1)

    def remote(src, dst, send, recv, device):
        return pltpu.make_async_remote_copy(
            src_ref=src, dst_ref=dst, send_sem=send, recv_sem=recv,
            device_id=device, device_id_type=MESH,
        )

    def a_rows(block, j):
        return a_all.at[pl.ds(pl.multiple_of(block * rows + j * CHUNK, CHUNK), CHUNK)]

    def direct(j, owner, send, recv, device):
        src = amp.at[pl.ds(j * CHUNK, CHUNK)]
        return remote(src, a_rows(owner, j), send.at[j], recv.at[j], device)

    def forward(j, s, owner, send, recv, device):
        block = a_rows(owner, j)
        return remote(block, block, send.at[s], recv.at[s], device)

    def v_block(col):
        return v_all.at[pl.ds(col * slots, slots)]

    def own_v(send, recv, device):
        return remote(ints, v_block(c), send, recv, device)

    def pass_v(col, send, recv, device):
        return remote(v_block(col), v_block(col), send, recv, device)

    def code_copy(owner, peer):
        return remote(codes_in, codes.at[owner], code_send.at[peer], code_recv.at[owner], (r, peer))

    for d in range(1, n_col):
        code_copy(c, (c + d) % n_col).start()
    for i in range(half):
        direct(i, r, xs, xr, (xn, c)).start()
        direct(half + i, r, ys, yr, (yn, c)).start()

    @pl.when(z < n_z - 1)
    def _():
        own_v(up_s.at[z], line_r.at[z], (r, c + 2)).start()

    @pl.when(z > 0)
    def _():
        own_v(down_s.at[z], line_r.at[z], (r, c - 2)).start()

    own_v(sib_s.at[z], sib_r.at[z], (r, sib)).start()
    for i in range(half):
        direct(half + i, r, xs, xr, (xn, c)).start()
        direct(i, r, ys, yr, (yn, c)).start()

    own_a = pltpu.make_async_copy(
        amp, a_all.at[pl.ds(pl.multiple_of(r * rows, CHUNK), rows)], own_sem.at[0]
    )
    keep_v = pltpu.make_async_copy(ints, v_block(c), own_sem.at[1])
    keep_code = pltpu.make_async_copy(codes_in, codes.at[c], own_sem.at[2])
    own_a.start()
    keep_v.start()
    keep_code.start()
    v_all[empty] = jnp.zeros((TILE, TILE), jnp.bfloat16)

    keep_code.wait()
    for d in range(1, n_col):
        other = (c + d) % n_col
        code_copy(other, other).wait_recv()
    lane = lax.broadcasted_iota(jnp.int32, (slots, TILE), 1)
    step = lax.broadcasted_iota(jnp.int32, (slots, TILE), 0)
    for t in range(row_tiles):
        found = jnp.full((slots, TILE), empty, jnp.int32)
        for col in range(n_col):
            hit = codes[col] == lane + t * TILE
            found = jnp.minimum(found, jnp.where(hit, step + col * slots, empty))
        place[t : t + 1, :] = jnp.min(found, axis=0, keepdims=True)
    to_scalar = pltpu.make_async_copy(place, place_s, own_sem.at[3])
    to_scalar.start()

    def forward_a(i):
        direct(i, xn, xs, xr, (xn, c)).wait_recv()
        forward(i, i, xn, fys, fyr, (yn, c)).start()
        direct(half + i, yn, ys, yr, (yn, c)).wait_recv()
        forward(half + i, i, yn, fxs, fxr, (xn, c)).start()

    def forward_v(d):
        @pl.when(z >= d)
        def _():
            b = z - d
            col = b * 2 + core
            pass_v(col, up_s.at[b], line_r.at[b], (r, c)).wait_recv()

            @pl.when(z < n_z - 1)
            def _():
                pass_v(col, up_s.at[b], line_r.at[b], (r, c + 2)).start()

            pass_v(col, sib_s.at[b], sib_r.at[b], (r, sib)).start()

        @pl.when(z + d < n_z)
        def _():
            b = z + d
            col = b * 2 + core
            pass_v(col, down_s.at[b], line_r.at[b], (r, c)).wait_recv()

            @pl.when(z > 0)
            def _():
                pass_v(col, down_s.at[b], line_r.at[b], (r, c - 2)).start()

            pass_v(col, sib_s.at[b], sib_r.at[b], (r, sib)).start()

    for i in range(half):
        forward_a(i)
        if i == 2:
            forward_v(1)
        if i == 4:
            forward_v(2)
    forward_v(3)
    keep_v.wait()
    for b in range(n_z):
        col = b * 2 + 1 - core
        pass_v(col, sib_s.at[b], sib_r.at[b], (r, sib)).wait_recv()
    to_scalar.wait()
    own_a.wait()

    def product(parts, first=False, last=False):
        def group(g, carry):
            top = pl.multiple_of(g * (GROUP * TILE), TILE)
            spot = 0
            for start, depth in parts:
                for k in range(depth // TILE):
                    tile_col = start // TILE + k
                    for t in range(GROUP):
                        lhs[t * TILE : (t + 1) * TILE, spot : spot + TILE] = v_all[
                            place_s[g * GROUP + t, tile_col]
                        ]
                    spot += TILE
            for n in range(0, width, WIDE):
                total = None
                spot = 0
                for start, depth in parts:
                    term = jnp.dot(
                        lhs[:, spot : spot + depth],
                        a_all[pl.ds(pl.multiple_of(start, CHUNK), depth), n : n + WIDE],
                        preferred_element_type=jnp.float32,
                    )
                    total = term if total is None else total + term
                    spot += depth
                here = (pl.ds(top, GROUP * TILE), slice(n, n + WIDE))
                if not first:
                    total = total + acc[here]
                if last:
                    stage[here] = total.astype(jnp.bfloat16)
                else:
                    acc[here] = total
            if last:
                out_copy(g).start()
            return carry

        lax.fori_loop(0, row_tiles // GROUP, group, 0)

    def out_copy(g):
        span = pl.ds(pl.multiple_of(g * (GROUP * TILE), TILE), GROUP * TILE)
        return pltpu.make_async_copy(stage.at[span], out.at[span], out_sem.at[g])

    part = half * CHUNK
    product([(r * rows, part)], first=True)
    product([(r * rows + part, part)])
    product([(xn * rows, part)])
    product([(yn * rows + part, part)])

    for i in range(half):
        direct(half + i, xn, xs, xr, (xn, c)).wait_recv()
    product([(xn * rows + part, part)])
    for i in range(half):
        direct(i, yn, ys, yr, (yn, c)).wait_recv()
    product([(yn * rows, part)])

    def diagonal(i, last):
        forward(i, i, dg, fys, fyr, (yn, c)).wait_recv()
        forward(half + i, i, dg, fxs, fxr, (xn, c)).wait_recv()
        first = dg * rows + i * CHUNK
        product([(first, CHUNK), (first + part, CHUNK)], last=last)

    def diagonal_step(i, carry):
        diagonal(i, False)
        return carry

    lax.fori_loop(0, half - 1, diagonal_step, 0)
    diagonal(half - 1, True)

    for d in range(1, n_col):
        code_copy(c, (c + d) % n_col).wait_send()
    for j in range(chunks):
        direct(j, r, xs, xr, (xn, c)).wait_send()
        direct(j, r, ys, yr, (yn, c)).wait_send()
    for i in range(half):
        forward(i, i, xn, fys, fyr, (yn, c)).wait_send()
        forward(half + i, i, yn, fxs, fxr, (xn, c)).wait_send()
    for b in range(n_z):
        col = b * 2 + core

        @pl.when((b <= z) & (z < n_z - 1))
        def _():
            pass_v(col, up_s.at[b], line_r.at[b], (r, c + 2)).wait_send()

        @pl.when((b >= z) & (z > 0))
        def _():
            pass_v(col, down_s.at[b], line_r.at[b], (r, c - 2)).wait_send()

        pass_v(col, sib_s.at[b], sib_r.at[b], (r, sib)).wait_send()
    for g in range(row_tiles // GROUP):
        out_copy(g).wait()


def ladder_body(n_row, n_col):
    def body(amplitudes, integrals, tile_ab, tile_cd):
        rows, width = amplitudes.shape
        slots = integrals.shape[0]
        chunks = rows // CHUNK
        half = chunks // 2
        row_tiles = rows // TILE
        code = jnp.where(tile_ab >= 0, tile_ab * TILE + tile_cd, -1)
        code = jnp.broadcast_to(code[:, None], (slots, TILE))
        dma = pltpu.SemaphoreType.DMA
        place_rows = -(-row_tiles // 8) * 8
        depth = n_row * rows
        return pl.pallas_call(
            ladder_kernel,
            out_shape=jax.ShapeDtypeStruct((rows, width), jnp.bfloat16),
            in_specs=[pl.BlockSpec(memory_space=pl.ANY)] * 3,
            out_specs=pl.BlockSpec(memory_space=pl.ANY),
            scratch_shapes=[
                pltpu.VMEM((depth, width), jnp.bfloat16),
                pltpu.VMEM((n_col * slots + 1, TILE, TILE), jnp.bfloat16),
                pltpu.VMEM((n_col, slots, TILE), jnp.int32),
                pltpu.VMEM((place_rows, TILE), jnp.int32),
                pltpu.SMEM((place_rows, TILE), jnp.int32),
                pltpu.VMEM((GROUP * TILE, half * CHUNK), jnp.bfloat16),
                pltpu.VMEM((rows, width), jnp.float32),
                pltpu.VMEM((rows, width), jnp.bfloat16),
                dma((4,)),
                dma((n_col,)),
                dma((n_col,)),
                dma((chunks,)),
                dma((chunks,)),
                dma((chunks,)),
                dma((chunks,)),
                dma((half,)),
                dma((half,)),
                dma((half,)),
                dma((half,)),
                dma((n_col // 2,)),
                dma((n_col // 2,)),
                dma((n_col // 2,)),
                dma((n_col // 2,)),
                dma((n_col // 2,)),
                dma((row_tiles // GROUP,)),
            ],
            compiler_params=pltpu.CompilerParams(
                collective_id=0, has_side_effects=True, vmem_limit_bytes=60 * 2**20
            ),
            cost_estimate=pl.CostEstimate(
                flops=2 * rows * depth * width,
                bytes_accessed=4 * rows * width,
                transcendentals=0,
            ),
        )(amplitudes, integrals, code)

    return body


def solution(mesh):
    in_specs = (
        P("row", "col"),
        P(("row", "col"), None, None),
        P(("row", "col")),
        P(("row", "col")),
    )
    out_specs = P("row", "col")
    n_row, n_col = mesh.shape["row"], mesh.shape["col"]
    body = ladder_body(n_row, n_col) if (n_row, n_col) == (4, 8) else plain_body
    return jax.shard_map(body, mesh=mesh, in_specs=in_specs, out_specs=out_specs, check_vma=False)
```

```python
import jax
import jax.numpy as jnp
from jax import lax
from jax.experimental import pallas as pl
from jax.experimental.pallas import tpu as pltpu
from jax.sharding import PartitionSpec as P

TILE = 128
NV = 80
MESH = pl.DeviceIdType.MESH
CHUNK = 256
GROUP = 5
WIDE = 256


def place_tiles(dense_block, pieces):
    tile_data, ab_code, cd_code = pieces
    ab_index = ab_code.astype(jnp.int32)
    cd_index = cd_code.astype(jnp.int32)
    position = jnp.where(ab_index >= 0, ab_index * NV + cd_index, dense_block.shape[0])
    return dense_block.at[position].add(tile_data, mode="drop")


def plain_body(amplitudes, integrals, tile_ab, tile_cd):
    row_tiles = amplitudes.shape[0] // TILE
    ab_code = tile_ab.astype(jnp.bfloat16)
    cd_code = tile_cd.astype(jnp.bfloat16)
    empty_block = jnp.zeros((row_tiles * NV, TILE, TILE), jnp.bfloat16)
    dense_block = place_tiles(
        empty_block,
        (
            lax.all_gather(integrals, "col", axis=0, tiled=True),
            lax.all_gather(ab_code, "col", axis=0, tiled=True),
            lax.all_gather(cd_code, "col", axis=0, tiled=True),
        ),
    )
    matrix = (
        dense_block.reshape(row_tiles, NV, TILE, TILE)
        .transpose(0, 2, 1, 3)
        .reshape(row_tiles * TILE, NV * TILE)
    )
    result = jnp.dot(
        matrix,
        lax.all_gather(amplitudes, "row", axis=0, tiled=True),
        preferred_element_type=jnp.float32,
    )
    return result.astype(jnp.bfloat16)


def ladder_kernel(
    amp, ints, tile_ab, tile_cd, out, a_all, v_all, codes_in, codes, place, place_s, lhs, acc,
    own_sem, code_send, code_recv, xs, xr, ys, yr, fxs, fxr, fys, fyr,
    up_s, down_s, line_r, sib_s, sib_r,
):
    rows, width = amp.shape
    slots = ints.shape[0]
    chunks = rows // CHUNK
    half = chunks // 2
    row_tiles = rows // TILE
    n_col = codes.shape[0]
    n_z = n_col // 2
    empty = n_col * slots

    r = lax.axis_index("row")
    c = lax.axis_index("col")
    x, y = r % 2, r // 2
    xn, yn, dg = r + 1 - 2 * x, r + 2 - 4 * y, 3 - r
    z, core = c // 2, c % 2
    sib = c + 1 - 2 * core

    barrier = pltpu.get_barrier_semaphore()
    for row in (xn, yn):
        pl.semaphore_signal(barrier, inc=1, device_id=(row, c), device_id_type=MESH)
    for d in range(1, n_col):
        pl.semaphore_signal(barrier, inc=1, device_id=(r, (c + d) % n_col), device_id_type=MESH)
    pl.semaphore_wait(barrier, n_col + 1)

    def remote(src, dst, send, recv, device):
        return pltpu.make_async_remote_copy(
            src_ref=src, dst_ref=dst, send_sem=send, recv_sem=recv,
            device_id=device, device_id_type=MESH,
        )

    def a_rows(block, j):
        return a_all.at[pl.ds(pl.multiple_of(block * rows + j * CHUNK, CHUNK), CHUNK)]

    def direct(j, owner, send, recv, device):
        src = amp.at[pl.ds(j * CHUNK, CHUNK)]
        return remote(src, a_rows(owner, j), send.at[j], recv.at[j], device)

    def forward(j, s, owner, send, recv, device):
        block = a_rows(owner, j)
        return remote(block, block, send.at[s], recv.at[s], device)

    def v_block(col):
        return v_all.at[pl.ds(col * slots, slots)]

    def own_v(send, recv, device):
        return remote(ints, v_block(c), send, recv, device)

    def pass_v(col, send, recv, device):
        return remote(v_block(col), v_block(col), send, recv, device)

    def code_copy(owner, peer):
        return remote(codes_in, codes.at[owner], code_send.at[peer], code_recv.at[owner], (r, peer))

    for i in range(half):
        direct(i, r, xs, xr, (xn, c)).start()
        direct(half + i, r, ys, yr, (yn, c)).start()

    @pl.when(z < n_z - 1)
    def _():
        own_v(up_s.at[z], line_r.at[z], (r, c + 2)).start()

    @pl.when(z > 0)
    def _():
        own_v(down_s.at[z], line_r.at[z], (r, c - 2)).start()

    own_v(sib_s.at[z], sib_r.at[z], (r, sib)).start()
    for s in range(slots):
        code = tile_ab[s] * TILE + tile_cd[s]
        codes_in[s : s + 1, :] = jnp.full((1, TILE), code, jnp.int32)
    for d in range(1, n_col):
        code_copy(c, (c + d) % n_col).start()
    for i in range(half):
        direct(half + i, r, xs, xr, (xn, c)).start()
        direct(i, r, ys, yr, (yn, c)).start()

    own_a = pltpu.make_async_copy(
        amp, a_all.at[pl.ds(pl.multiple_of(r * rows, CHUNK), rows)], own_sem.at[0]
    )
    keep_v = pltpu.make_async_copy(ints, v_block(c), own_sem.at[1])
    keep_code = pltpu.make_async_copy(codes_in, codes.at[c], own_sem.at[2])
    own_a.start()
    keep_v.start()
    keep_code.start()
    v_all[empty] = jnp.zeros((TILE, TILE), jnp.bfloat16)

    keep_code.wait()
    for d in range(1, n_col):
        other = (c + d) % n_col
        code_copy(other, other).wait_recv()
    lane = lax.broadcasted_iota(jnp.int32, (slots, TILE), 1)
    step = lax.broadcasted_iota(jnp.int32, (slots, TILE), 0)
    for t in range(row_tiles):
        found = jnp.full((slots, TILE), empty, jnp.int32)
        for col in range(n_col):
            hit = codes[col] == lane + t * TILE
            found = jnp.minimum(found, jnp.where(hit, step + col * slots, empty))
        place[t : t + 1, :] = jnp.min(found, axis=0, keepdims=True)
    to_scalar = pltpu.make_async_copy(place, place_s, own_sem.at[3])
    to_scalar.start()

    def forward_a(i):
        direct(i, xn, xs, xr, (xn, c)).wait_recv()
        forward(i, i, xn, fys, fyr, (yn, c)).start()
        direct(half + i, yn, ys, yr, (yn, c)).wait_recv()
        forward(half + i, i, yn, fxs, fxr, (xn, c)).start()

    def forward_v(d):
        @pl.when(z >= d)
        def _():
            b = z - d
            col = b * 2 + core
            pass_v(col, up_s.at[b], line_r.at[b], (r, c)).wait_recv()

            @pl.when(z < n_z - 1)
            def _():
                pass_v(col, up_s.at[b], line_r.at[b], (r, c + 2)).start()

            pass_v(col, sib_s.at[b], sib_r.at[b], (r, sib)).start()

        @pl.when(z + d < n_z)
        def _():
            b = z + d
            col = b * 2 + core
            pass_v(col, down_s.at[b], line_r.at[b], (r, c)).wait_recv()

            @pl.when(z > 0)
            def _():
                pass_v(col, down_s.at[b], line_r.at[b], (r, c - 2)).start()

            pass_v(col, sib_s.at[b], sib_r.at[b], (r, sib)).start()

    for i in range(half):
        forward_a(i)
        if i == 2:
            forward_v(1)
        if i == 4:
            forward_v(2)
    forward_v(3)
    keep_v.wait()
    for b in range(n_z):
        col = b * 2 + 1 - core
        pass_v(col, sib_s.at[b], sib_r.at[b], (r, sib)).wait_recv()
    to_scalar.wait()
    own_a.wait()

    def product(parts, first=False, last=False):
        def group(g, carry):
            top = pl.multiple_of(g * (GROUP * TILE), TILE)
            spot = 0
            for start, depth in parts:
                for k in range(depth // TILE):
                    tile_col = start // TILE + k
                    for t in range(GROUP):
                        lhs[t * TILE : (t + 1) * TILE, spot : spot + TILE] = v_all[
                            place_s[g * GROUP + t, tile_col]
                        ]
                    spot += TILE
            for n in range(0, width, WIDE):
                total = None
                spot = 0
                for start, depth in parts:
                    term = jnp.dot(
                        lhs[:, spot : spot + depth],
                        a_all[pl.ds(pl.multiple_of(start, CHUNK), depth), n : n + WIDE],
                        preferred_element_type=jnp.float32,
                    )
                    total = term if total is None else total + term
                    spot += depth
                here = (pl.ds(top, GROUP * TILE), slice(n, n + WIDE))
                if not first:
                    total = total + acc[here]
                if last:
                    out[here] = total.astype(jnp.bfloat16)
                else:
                    acc[here] = total
            return carry

        lax.fori_loop(0, row_tiles // GROUP, group, 0)

    part = half * CHUNK
    product([(r * rows, part)], first=True)
    product([(r * rows + part, part)])
    product([(xn * rows, part)])
    product([(yn * rows + part, part)])

    for i in range(half):
        direct(half + i, xn, xs, xr, (xn, c)).wait_recv()
    product([(xn * rows + part, part)])
    for i in range(half):
        direct(i, yn, ys, yr, (yn, c)).wait_recv()
    product([(yn * rows, part)])

    def diagonal(i, last):
        forward(i, i, dg, fys, fyr, (yn, c)).wait_recv()
        forward(half + i, i, dg, fxs, fxr, (xn, c)).wait_recv()
        first = dg * rows + i * CHUNK
        product([(first, CHUNK), (first + part, CHUNK)], last=last)

    def diagonal_step(i, carry):
        diagonal(i, False)
        return carry

    lax.fori_loop(0, half - 1, diagonal_step, 0)
    diagonal(half - 1, True)

    for d in range(1, n_col):
        code_copy(c, (c + d) % n_col).wait_send()
    for j in range(chunks):
        direct(j, r, xs, xr, (xn, c)).wait_send()
        direct(j, r, ys, yr, (yn, c)).wait_send()
    for i in range(half):
        forward(i, i, xn, fys, fyr, (yn, c)).wait_send()
        forward(half + i, i, yn, fxs, fxr, (xn, c)).wait_send()
    for b in range(n_z):
        col = b * 2 + core

        @pl.when((b <= z) & (z < n_z - 1))
        def _():
            pass_v(col, up_s.at[b], line_r.at[b], (r, c + 2)).wait_send()

        @pl.when((b >= z) & (z > 0))
        def _():
            pass_v(col, down_s.at[b], line_r.at[b], (r, c - 2)).wait_send()

        pass_v(col, sib_s.at[b], sib_r.at[b], (r, sib)).wait_send()


def ladder_body(n_row, n_col):
    def body(amplitudes, integrals, tile_ab, tile_cd):
        rows, width = amplitudes.shape
        slots = integrals.shape[0]
        chunks = rows // CHUNK
        half = chunks // 2
        row_tiles = rows // TILE
        dma = pltpu.SemaphoreType.DMA
        place_rows = -(-row_tiles // 8) * 8
        depth = n_row * rows
        return pl.pallas_call(
            ladder_kernel,
            out_shape=pltpu.VMEM((rows, width), jnp.bfloat16),
            in_specs=[pl.BlockSpec(memory_space=pl.ANY)] * 2 + [pl.BlockSpec(memory_space=pltpu.SMEM)] * 2,
            out_specs=pl.BlockSpec(memory_space=pltpu.VMEM),
            scratch_shapes=[
                pltpu.VMEM((depth, width), jnp.bfloat16),
                pltpu.VMEM((n_col * slots + 1, TILE, TILE), jnp.bfloat16),
                pltpu.VMEM((slots, TILE), jnp.int32),
                pltpu.VMEM((n_col, slots, TILE), jnp.int32),
                pltpu.VMEM((place_rows, TILE), jnp.int32),
                pltpu.SMEM((place_rows, TILE), jnp.int32),
                pltpu.VMEM((GROUP * TILE, half * CHUNK), jnp.bfloat16),
                pltpu.VMEM((rows, width), jnp.float32),
                dma((4,)),
                dma((n_col,)),
                dma((n_col,)),
                dma((chunks,)),
                dma((chunks,)),
                dma((chunks,)),
                dma((chunks,)),
                dma((half,)),
                dma((half,)),
                dma((half,)),
                dma((half,)),
                dma((n_col // 2,)),
                dma((n_col // 2,)),
                dma((n_col // 2,)),
                dma((n_col // 2,)),
                dma((n_col // 2,)),
            ],
            compiler_params=pltpu.CompilerParams(
                collective_id=0, has_side_effects=True, vmem_limit_bytes=50 * 2**20
            ),
            cost_estimate=pl.CostEstimate(
                flops=2 * rows * depth * width,
                bytes_accessed=4 * rows * width,
                transcendentals=0,
            ),
        )(amplitudes, integrals, tile_ab, tile_cd)

    return body


def solution(mesh):
    in_specs = (
        P("row", "col"),
        P(("row", "col"), None, None),
        P(("row", "col")),
        P(("row", "col")),
    )
    out_specs = P("row", "col")
    n_row, n_col = mesh.shape["row"], mesh.shape["col"]
    body = ladder_body(n_row, n_col) if (n_row, n_col) == (4, 8) else plain_body
    return jax.shard_map(body, mesh=mesh, in_specs=in_specs, out_specs=out_specs, check_vma=False)
```

```python
import jax
import jax.numpy as jnp
from jax import lax
from jax.experimental import pallas as pl
from jax.experimental.pallas import tpu as pltpu
from jax.sharding import PartitionSpec as P

TILE = 128
NV = 80
MESH = pl.DeviceIdType.MESH
CHUNK = 256
GROUP = 5
WIDE = 256


def place_tiles(dense_block, pieces):
    tile_data, ab_code, cd_code = pieces
    ab_index = ab_code.astype(jnp.int32)
    cd_index = cd_code.astype(jnp.int32)
    position = jnp.where(ab_index >= 0, ab_index * NV + cd_index, dense_block.shape[0])
    return dense_block.at[position].add(tile_data, mode="drop")


def plain_body(amplitudes, integrals, tile_ab, tile_cd):
    row_tiles = amplitudes.shape[0] // TILE
    ab_code = tile_ab.astype(jnp.bfloat16)
    cd_code = tile_cd.astype(jnp.bfloat16)
    empty_block = jnp.zeros((row_tiles * NV, TILE, TILE), jnp.bfloat16)
    dense_block = place_tiles(
        empty_block,
        (
            lax.all_gather(integrals, "col", axis=0, tiled=True),
            lax.all_gather(ab_code, "col", axis=0, tiled=True),
            lax.all_gather(cd_code, "col", axis=0, tiled=True),
        ),
    )
    matrix = (
        dense_block.reshape(row_tiles, NV, TILE, TILE)
        .transpose(0, 2, 1, 3)
        .reshape(row_tiles * TILE, NV * TILE)
    )
    result = jnp.dot(
        matrix,
        lax.all_gather(amplitudes, "row", axis=0, tiled=True),
        preferred_element_type=jnp.float32,
    )
    return result.astype(jnp.bfloat16)


def ladder_kernel(
    amp, ints, tile_ab, tile_cd, out, a_all, v_all, codes_in, codes, place, place_s, lhs, acc,
    own_sem, code_send, code_recv, xs, xr, ys, yr, fxs, fxr, fys, fyr,
    up_s, down_s, line_r, sib_s, sib_r,
):
    rows, width = amp.shape
    slots = ints.shape[0]
    chunks = rows // CHUNK
    half = chunks // 2
    row_tiles = rows // TILE
    n_col = codes.shape[0]
    n_z = n_col // 2
    empty = n_col * slots

    r = lax.axis_index("row")
    c = lax.axis_index("col")
    x, y = r % 2, r // 2
    xn, yn, dg = r + 1 - 2 * x, r + 2 - 4 * y, 3 - r
    z, core = c // 2, c % 2
    sib = c + 1 - 2 * core

    barrier = pltpu.get_barrier_semaphore()
    for row in (xn, yn):
        pl.semaphore_signal(barrier, inc=1, device_id=(row, c), device_id_type=MESH)
    for d in range(1, n_col):
        pl.semaphore_signal(barrier, inc=1, device_id=(r, (c + d) % n_col), device_id_type=MESH)
    pl.semaphore_wait(barrier, n_col + 1)

    def remote(src, dst, send, recv, device):
        return pltpu.make_async_remote_copy(
            src_ref=src, dst_ref=dst, send_sem=send, recv_sem=recv,
            device_id=device, device_id_type=MESH,
        )

    def a_rows(block, j):
        return a_all.at[pl.ds(pl.multiple_of(block * rows + j * CHUNK, CHUNK), CHUNK)]

    def direct(j, owner, send, recv, device):
        src = amp.at[pl.ds(j * CHUNK, CHUNK)]
        return remote(src, a_rows(owner, j), send.at[j], recv.at[j], device)

    def forward(j, s, owner, send, recv, device):
        block = a_rows(owner, j)
        return remote(block, block, send.at[s], recv.at[s], device)

    def v_block(col):
        return v_all.at[pl.ds(col * slots, slots)]

    def own_v(send, recv, device):
        return remote(ints, v_block(c), send, recv, device)

    def pass_v(col, send, recv, device):
        return remote(v_block(col), v_block(col), send, recv, device)

    def code_copy(owner, peer):
        return remote(codes_in, codes.at[owner], code_send.at[peer], code_recv.at[owner], (r, peer))

    for i in range(half):
        direct(i, r, xs, xr, (xn, c)).start()
        direct(half + i, r, ys, yr, (yn, c)).start()

    @pl.when(z < n_z - 1)
    def _():
        own_v(up_s.at[z], line_r.at[z], (r, c + 2)).start()

    @pl.when(z > 0)
    def _():
        own_v(down_s.at[z], line_r.at[z], (r, c - 2)).start()

    own_v(sib_s.at[z], sib_r.at[z], (r, sib)).start()
    for s in range(slots):
        code = tile_ab[s] * TILE + tile_cd[s]
        codes_in[s : s + 1, :] = jnp.full((1, TILE), code, jnp.int32)
    for d in range(1, n_col):
        code_copy(c, (c + d) % n_col).start()
    for i in range(half):
        direct(half + i, r, xs, xr, (xn, c)).start()
        direct(i, r, ys, yr, (yn, c)).start()

    own_a = pltpu.make_async_copy(
        amp, a_all.at[pl.ds(pl.multiple_of(r * rows, CHUNK), rows)], own_sem.at[0]
    )
    keep_v = pltpu.make_async_copy(ints, v_block(c), own_sem.at[1])
    keep_code = pltpu.make_async_copy(codes_in, codes.at[c], own_sem.at[2])
    own_a.start()
    keep_v.start()
    keep_code.start()
    v_all[empty] = jnp.zeros((TILE, TILE), jnp.bfloat16)

    keep_code.wait()
    for d in range(1, n_col):
        other = (c + d) % n_col
        code_copy(other, other).wait_recv()
    lane = lax.broadcasted_iota(jnp.int32, (slots, TILE), 1)
    step = lax.broadcasted_iota(jnp.int32, (slots, TILE), 0)
    for t in range(row_tiles):
        found = jnp.full((slots, TILE), empty, jnp.int32)
        for col in range(n_col):
            hit = codes[col] == lane + t * TILE
            found = jnp.minimum(found, jnp.where(hit, step + col * slots, empty))
        place[t : t + 1, :] = jnp.min(found, axis=0, keepdims=True)
    to_scalar = pltpu.make_async_copy(place, place_s, own_sem.at[3])
    to_scalar.start()

    def forward_a(i):
        direct(i, xn, xs, xr, (xn, c)).wait_recv()
        forward(i, i, xn, fys, fyr, (yn, c)).start()
        direct(half + i, yn, ys, yr, (yn, c)).wait_recv()
        forward(half + i, i, yn, fxs, fxr, (xn, c)).start()

    def forward_v(d):
        @pl.when(z >= d)
        def _():
            b = z - d
            col = b * 2 + core
            pass_v(col, up_s.at[b], line_r.at[b], (r, c)).wait_recv()

            @pl.when(z < n_z - 1)
            def _():
                pass_v(col, up_s.at[b], line_r.at[b], (r, c + 2)).start()

            pass_v(col, sib_s.at[b], sib_r.at[b], (r, sib)).start()

        @pl.when(z + d < n_z)
        def _():
            b = z + d
            col = b * 2 + core
            pass_v(col, down_s.at[b], line_r.at[b], (r, c)).wait_recv()

            @pl.when(z > 0)
            def _():
                pass_v(col, down_s.at[b], line_r.at[b], (r, c - 2)).start()

            pass_v(col, sib_s.at[b], sib_r.at[b], (r, sib)).start()

    for i in range(half):
        forward_a(i)
        if i == 2:
            forward_v(1)
        if i == 4:
            forward_v(2)
    forward_v(3)
    keep_v.wait()
    for b in range(n_z):
        col = b * 2 + 1 - core
        pass_v(col, sib_s.at[b], sib_r.at[b], (r, sib)).wait_recv()
    to_scalar.wait()
    own_a.wait()

    def product(parts, first=False, last=False):
        def group(g, carry):
            top = pl.multiple_of(g * (GROUP * TILE), TILE)
            spot = 0
            for start, depth in parts:
                for k in range(depth // TILE):
                    tile_col = start // TILE + k
                    for t in range(GROUP):
                        lhs[t * TILE : (t + 1) * TILE, spot : spot + TILE] = v_all[
                            place_s[g * GROUP + t, tile_col]
                        ]
                    spot += TILE
            for n in range(0, width, WIDE):
                total = None
                spot = 0
                for start, depth in parts:
                    term = jnp.dot(
                        lhs[:, spot : spot + depth],
                        a_all[pl.ds(pl.multiple_of(start, CHUNK), depth), n : n + WIDE],
                        preferred_element_type=jnp.float32,
                    )
                    total = term if total is None else total + term
                    spot += depth
                here = (pl.ds(top, GROUP * TILE), slice(n, n + WIDE))
                if not first:
                    total = total + acc[here]
                if last:
                    out[here] = total.astype(jnp.bfloat16)
                else:
                    acc[here] = total
            return carry

        lax.fori_loop(0, row_tiles // GROUP, group, 0)

    part = half * CHUNK
    product([(r * rows, part)], first=True)
    product([(r * rows + part, part)])
    product([(xn * rows, part)])
    product([(yn * rows + part, part)])

    for i in range(half):
        direct(half + i, xn, xs, xr, (xn, c)).wait_recv()
    product([(xn * rows + part, part)])
    for i in range(half):
        direct(i, yn, ys, yr, (yn, c)).wait_recv()
    product([(yn * rows, part)])

    def diagonal_step(i, carry):
        forward(i, i, dg, fys, fyr, (yn, c)).wait_recv()
        forward(half + i, i, dg, fxs, fxr, (xn, c)).wait_recv()
        first = dg * rows + i * CHUNK
        product([(first, CHUNK), (first + part, CHUNK)])
        return carry

    lax.fori_loop(0, half - 1, diagonal_step, 0)
    end = half - 1
    forward(end, end, dg, fys, fyr, (yn, c)).wait_recv()
    product([(dg * rows + end * CHUNK, CHUNK)])
    forward(half + end, end, dg, fxs, fxr, (xn, c)).wait_recv()
    product([(dg * rows + part + end * CHUNK, CHUNK)], last=True)

    for d in range(1, n_col):
        code_copy(c, (c + d) % n_col).wait_send()
    for j in range(chunks):
        direct(j, r, xs, xr, (xn, c)).wait_send()
        direct(j, r, ys, yr, (yn, c)).wait_send()
    for i in range(half):
        forward(i, i, xn, fys, fyr, (yn, c)).wait_send()
        forward(half + i, i, yn, fxs, fxr, (xn, c)).wait_send()
    for b in range(n_z):
        col = b * 2 + core

        @pl.when((b <= z) & (z < n_z - 1))
        def _():
            pass_v(col, up_s.at[b], line_r.at[b], (r, c + 2)).wait_send()

        @pl.when((b >= z) & (z > 0))
        def _():
            pass_v(col, down_s.at[b], line_r.at[b], (r, c - 2)).wait_send()

        pass_v(col, sib_s.at[b], sib_r.at[b], (r, sib)).wait_send()


def ladder_body(n_row, n_col):
    def body(amplitudes, integrals, tile_ab, tile_cd):
        rows, width = amplitudes.shape
        slots = integrals.shape[0]
        chunks = rows // CHUNK
        half = chunks // 2
        row_tiles = rows // TILE
        dma = pltpu.SemaphoreType.DMA
        place_rows = -(-row_tiles // 8) * 8
        depth = n_row * rows
        return pl.pallas_call(
            ladder_kernel,
            out_shape=pltpu.VMEM((rows, width), jnp.bfloat16),
            in_specs=[pl.BlockSpec(memory_space=pl.ANY)] * 2 + [pl.BlockSpec(memory_space=pltpu.SMEM)] * 2,
            out_specs=pl.BlockSpec(memory_space=pltpu.VMEM),
            scratch_shapes=[
                pltpu.VMEM((depth, width), jnp.bfloat16),
                pltpu.VMEM((n_col * slots + 1, TILE, TILE), jnp.bfloat16),
                pltpu.VMEM((slots, TILE), jnp.int32),
                pltpu.VMEM((n_col, slots, TILE), jnp.int32),
                pltpu.VMEM((place_rows, TILE), jnp.int32),
                pltpu.SMEM((place_rows, TILE), jnp.int32),
                pltpu.VMEM((GROUP * TILE, half * CHUNK), jnp.bfloat16),
                pltpu.VMEM((rows, width), jnp.float32),
                dma((4,)),
                dma((n_col,)),
                dma((n_col,)),
                dma((chunks,)),
                dma((chunks,)),
                dma((chunks,)),
                dma((chunks,)),
                dma((half,)),
                dma((half,)),
                dma((half,)),
                dma((half,)),
                dma((n_col // 2,)),
                dma((n_col // 2,)),
                dma((n_col // 2,)),
                dma((n_col // 2,)),
                dma((n_col // 2,)),
            ],
            compiler_params=pltpu.CompilerParams(
                collective_id=0, has_side_effects=True, vmem_limit_bytes=50 * 2**20
            ),
            cost_estimate=pl.CostEstimate(
                flops=2 * rows * depth * width,
                bytes_accessed=4 * rows * width,
                transcendentals=0,
            ),
        )(amplitudes, integrals, tile_ab, tile_cd)

    return body


def solution(mesh):
    in_specs = (
        P("row", "col"),
        P(("row", "col"), None, None),
        P(("row", "col")),
        P(("row", "col")),
    )
    out_specs = P("row", "col")
    n_row, n_col = mesh.shape["row"], mesh.shape["col"]
    body = ladder_body(n_row, n_col) if (n_row, n_col) == (4, 8) else plain_body
    return jax.shard_map(body, mesh=mesh, in_specs=in_specs, out_specs=out_specs, check_vma=False)
```

```python
import jax
import jax.numpy as jnp
from jax import lax
from jax.experimental import pallas as pl
from jax.experimental.pallas import tpu as pltpu
from jax.sharding import PartitionSpec as P

TILE = 128
NV = 80
MESH = pl.DeviceIdType.MESH
CHUNK = 256
GROUP = 5
WIDE = 256


def place_tiles(dense_block, pieces):
    tile_data, ab_code, cd_code = pieces
    ab_index = ab_code.astype(jnp.int32)
    cd_index = cd_code.astype(jnp.int32)
    position = jnp.where(ab_index >= 0, ab_index * NV + cd_index, dense_block.shape[0])
    return dense_block.at[position].add(tile_data, mode="drop")


def plain_body(amplitudes, integrals, tile_ab, tile_cd):
    row_tiles = amplitudes.shape[0] // TILE
    ab_code = tile_ab.astype(jnp.bfloat16)
    cd_code = tile_cd.astype(jnp.bfloat16)
    empty_block = jnp.zeros((row_tiles * NV, TILE, TILE), jnp.bfloat16)
    dense_block = place_tiles(
        empty_block,
        (
            lax.all_gather(integrals, "col", axis=0, tiled=True),
            lax.all_gather(ab_code, "col", axis=0, tiled=True),
            lax.all_gather(cd_code, "col", axis=0, tiled=True),
        ),
    )
    matrix = (
        dense_block.reshape(row_tiles, NV, TILE, TILE)
        .transpose(0, 2, 1, 3)
        .reshape(row_tiles * TILE, NV * TILE)
    )
    result = jnp.dot(
        matrix,
        lax.all_gather(amplitudes, "row", axis=0, tiled=True),
        preferred_element_type=jnp.float32,
    )
    return result.astype(jnp.bfloat16)


def ladder_kernel(
    amp, ints, tile_ab, tile_cd, out, a_all, v_all, codes_in, codes, place, place_s, lhs, lhs_end, acc,
    own_sem, code_send, code_recv, xs, xr, ys, yr, fxs, fxr, fys, fyr,
    up_s, down_s, line_r, sib_s, sib_r,
):
    rows, width = amp.shape
    slots = ints.shape[0]
    chunks = rows // CHUNK
    half = chunks // 2
    row_tiles = rows // TILE
    n_col = codes.shape[0]
    n_z = n_col // 2
    empty = n_col * slots

    r = lax.axis_index("row")
    c = lax.axis_index("col")
    x, y = r % 2, r // 2
    xn, yn, dg = r + 1 - 2 * x, r + 2 - 4 * y, 3 - r
    z, core = c // 2, c % 2
    sib = c + 1 - 2 * core

    barrier = pltpu.get_barrier_semaphore()
    for row in (xn, yn):
        pl.semaphore_signal(barrier, inc=1, device_id=(row, c), device_id_type=MESH)
    for d in range(1, n_col):
        pl.semaphore_signal(barrier, inc=1, device_id=(r, (c + d) % n_col), device_id_type=MESH)
    pl.semaphore_wait(barrier, n_col + 1)

    def remote(src, dst, send, recv, device):
        return pltpu.make_async_remote_copy(
            src_ref=src, dst_ref=dst, send_sem=send, recv_sem=recv,
            device_id=device, device_id_type=MESH,
        )

    def a_rows(block, j):
        return a_all.at[pl.ds(pl.multiple_of(block * rows + j * CHUNK, CHUNK), CHUNK)]

    def direct(j, owner, send, recv, device):
        src = amp.at[pl.ds(j * CHUNK, CHUNK)]
        return remote(src, a_rows(owner, j), send.at[j], recv.at[j], device)

    def forward(j, s, owner, send, recv, device):
        block = a_rows(owner, j)
        return remote(block, block, send.at[s], recv.at[s], device)

    def v_block(col):
        return v_all.at[pl.ds(col * slots, slots)]

    def own_v(send, recv, device):
        return remote(ints, v_block(c), send, recv, device)

    def pass_v(col, send, recv, device):
        return remote(v_block(col), v_block(col), send, recv, device)

    def code_copy(owner, peer):
        return remote(codes_in, codes.at[owner], code_send.at[peer], code_recv.at[owner], (r, peer))

    for i in range(half):
        direct(i, r, xs, xr, (xn, c)).start()
        direct(half + i, r, ys, yr, (yn, c)).start()

    @pl.when(z < n_z - 1)
    def _():
        own_v(up_s.at[z], line_r.at[z], (r, c + 2)).start()

    @pl.when(z > 0)
    def _():
        own_v(down_s.at[z], line_r.at[z], (r, c - 2)).start()

    own_v(sib_s.at[z], sib_r.at[z], (r, sib)).start()
    for s in range(slots):
        code = tile_ab[s] * TILE + tile_cd[s]
        codes_in[s : s + 1, :] = jnp.full((1, TILE), code, jnp.int32)
    for d in range(1, n_col):
        code_copy(c, (c + d) % n_col).start()
    for i in range(half):
        direct(half + i, r, xs, xr, (xn, c)).start()
        direct(i, r, ys, yr, (yn, c)).start()

    own_a = pltpu.make_async_copy(
        amp, a_all.at[pl.ds(pl.multiple_of(r * rows, CHUNK), rows)], own_sem.at[0]
    )
    keep_v = pltpu.make_async_copy(ints, v_block(c), own_sem.at[1])
    keep_code = pltpu.make_async_copy(codes_in, codes.at[c], own_sem.at[2])
    own_a.start()
    keep_v.start()
    keep_code.start()
    v_all[empty] = jnp.zeros((TILE, TILE), jnp.bfloat16)

    keep_code.wait()
    for d in range(1, n_col):
        other = (c + d) % n_col
        code_copy(other, other).wait_recv()
    lane = lax.broadcasted_iota(jnp.int32, (slots, TILE), 1)
    step = lax.broadcasted_iota(jnp.int32, (slots, TILE), 0)
    for t in range(row_tiles):
        found = jnp.full((slots, TILE), empty, jnp.int32)
        for col in range(n_col):
            hit = codes[col] == lane + t * TILE
            found = jnp.minimum(found, jnp.where(hit, step + col * slots, empty))
        place[t : t + 1, :] = jnp.min(found, axis=0, keepdims=True)
    to_scalar = pltpu.make_async_copy(place, place_s, own_sem.at[3])
    to_scalar.start()

    def forward_a(i):
        direct(i, xn, xs, xr, (xn, c)).wait_recv()
        forward(i, i, xn, fys, fyr, (yn, c)).start()
        direct(half + i, yn, ys, yr, (yn, c)).wait_recv()
        forward(half + i, i, yn, fxs, fxr, (xn, c)).start()

    def forward_v(d):
        @pl.when(z >= d)
        def _():
            b = z - d
            col = b * 2 + core
            pass_v(col, up_s.at[b], line_r.at[b], (r, c)).wait_recv()

            @pl.when(z < n_z - 1)
            def _():
                pass_v(col, up_s.at[b], line_r.at[b], (r, c + 2)).start()

            pass_v(col, sib_s.at[b], sib_r.at[b], (r, sib)).start()

        @pl.when(z + d < n_z)
        def _():
            b = z + d
            col = b * 2 + core
            pass_v(col, down_s.at[b], line_r.at[b], (r, c)).wait_recv()

            @pl.when(z > 0)
            def _():
                pass_v(col, down_s.at[b], line_r.at[b], (r, c - 2)).start()

            pass_v(col, sib_s.at[b], sib_r.at[b], (r, sib)).start()

    for i in range(half):
        forward_a(i)
        if i == 2:
            forward_v(1)
        if i == 4:
            forward_v(2)
    forward_v(3)
    keep_v.wait()
    for b in range(n_z):
        col = b * 2 + 1 - core
        pass_v(col, sib_s.at[b], sib_r.at[b], (r, sib)).wait_recv()
    to_scalar.wait()
    own_a.wait()

    def left(top, last):
        return lhs_end.at[pl.ds(top, GROUP * TILE)] if last else lhs

    def product(parts, first=False, last=False):
        def group(g, carry):
            top = pl.multiple_of(g * (GROUP * TILE), TILE)
            spot = 0
            for start, depth in [] if last else parts:
                for k in range(depth // TILE):
                    tile_col = start // TILE + k
                    for t in range(GROUP):
                        lhs[t * TILE : (t + 1) * TILE, spot : spot + TILE] = v_all[
                            place_s[g * GROUP + t, tile_col]
                        ]
                    spot += TILE
            for n in range(0, width, WIDE):
                total = None
                spot = 0
                for start, depth in parts:
                    term = jnp.dot(
                        left(top, last)[:, spot : spot + depth],
                        a_all[pl.ds(pl.multiple_of(start, CHUNK), depth), n : n + WIDE],
                        preferred_element_type=jnp.float32,
                    )
                    total = term if total is None else total + term
                    spot += depth
                here = (pl.ds(top, GROUP * TILE), slice(n, n + WIDE))
                if not first:
                    total = total + acc[here]
                if last:
                    out[here] = total.astype(jnp.bfloat16)
                else:
                    acc[here] = total
            return carry

        lax.fori_loop(0, row_tiles // GROUP, group, 0)

    part = half * CHUNK
    product([(r * rows, part)], first=True)
    product([(r * rows + part, part)])
    product([(xn * rows, part)])
    product([(yn * rows + part, part)])

    for i in range(half):
        direct(half + i, xn, xs, xr, (xn, c)).wait_recv()
    product([(xn * rows + part, part)])
    for i in range(half):
        direct(i, yn, ys, yr, (yn, c)).wait_recv()
    product([(yn * rows, part)])

    def diagonal(i, last):
        forward(i, i, dg, fys, fyr, (yn, c)).wait_recv()
        forward(half + i, i, dg, fxs, fxr, (xn, c)).wait_recv()
        first = dg * rows + i * CHUNK
        product([(first, CHUNK), (first + part, CHUNK)], last=last)

    def diagonal_step(i, carry):
        diagonal(i, False)
        return carry

    end = (dg * rows + (half - 1) * CHUNK) // TILE

    def read_end(t, carry):
        for k in range(2 * CHUNK // TILE):
            tile_col = end + k if k < CHUNK // TILE else end + part // TILE + k - CHUNK // TILE
            span = pl.ds(pl.multiple_of(t * TILE, TILE), TILE)
            lhs_end[span, k * TILE : (k + 1) * TILE] = v_all[place_s[t, tile_col]]
        return carry

    lax.fori_loop(0, row_tiles, read_end, 0)
    lax.fori_loop(0, half - 1, diagonal_step, 0)
    diagonal(half - 1, True)

    for d in range(1, n_col):
        code_copy(c, (c + d) % n_col).wait_send()
    for j in range(chunks):
        direct(j, r, xs, xr, (xn, c)).wait_send()
        direct(j, r, ys, yr, (yn, c)).wait_send()
    for i in range(half):
        forward(i, i, xn, fys, fyr, (yn, c)).wait_send()
        forward(half + i, i, yn, fxs, fxr, (xn, c)).wait_send()
    for b in range(n_z):
        col = b * 2 + core

        @pl.when((b <= z) & (z < n_z - 1))
        def _():
            pass_v(col, up_s.at[b], line_r.at[b], (r, c + 2)).wait_send()

        @pl.when((b >= z) & (z > 0))
        def _():
            pass_v(col, down_s.at[b], line_r.at[b], (r, c - 2)).wait_send()

        pass_v(col, sib_s.at[b], sib_r.at[b], (r, sib)).wait_send()


def ladder_body(n_row, n_col):
    def body(amplitudes, integrals, tile_ab, tile_cd):
        rows, width = amplitudes.shape
        slots = integrals.shape[0]
        chunks = rows // CHUNK
        half = chunks // 2
        row_tiles = rows // TILE
        dma = pltpu.SemaphoreType.DMA
        place_rows = -(-row_tiles // 8) * 8
        depth = n_row * rows
        return pl.pallas_call(
            ladder_kernel,
            out_shape=pltpu.VMEM((rows, width), jnp.bfloat16),
            in_specs=[pl.BlockSpec(memory_space=pl.ANY)] * 2 + [pl.BlockSpec(memory_space=pltpu.SMEM)] * 2,
            out_specs=pl.BlockSpec(memory_space=pltpu.VMEM),
            scratch_shapes=[
                pltpu.VMEM((depth, width), jnp.bfloat16),
                pltpu.VMEM((n_col * slots + 1, TILE, TILE), jnp.bfloat16),
                pltpu.VMEM((slots, TILE), jnp.int32),
                pltpu.VMEM((n_col, slots, TILE), jnp.int32),
                pltpu.VMEM((place_rows, TILE), jnp.int32),
                pltpu.SMEM((place_rows, TILE), jnp.int32),
                pltpu.VMEM((GROUP * TILE, half * CHUNK), jnp.bfloat16),
                pltpu.VMEM((rows, 2 * CHUNK), jnp.bfloat16),
                pltpu.VMEM((rows, width), jnp.float32),
                dma((4,)),
                dma((n_col,)),
                dma((n_col,)),
                dma((chunks,)),
                dma((chunks,)),
                dma((chunks,)),
                dma((chunks,)),
                dma((half,)),
                dma((half,)),
                dma((half,)),
                dma((half,)),
                dma((n_col // 2,)),
                dma((n_col // 2,)),
                dma((n_col // 2,)),
                dma((n_col // 2,)),
                dma((n_col // 2,)),
            ],
            compiler_params=pltpu.CompilerParams(
                collective_id=0, has_side_effects=True, vmem_limit_bytes=50 * 2**20
            ),
            cost_estimate=pl.CostEstimate(
                flops=2 * rows * depth * width,
                bytes_accessed=4 * rows * width,
                transcendentals=0,
            ),
        )(amplitudes, integrals, tile_ab, tile_cd)

    return body


def solution(mesh):
    in_specs = (
        P("row", "col"),
        P(("row", "col"), None, None),
        P(("row", "col")),
        P(("row", "col")),
    )
    out_specs = P("row", "col")
    n_row, n_col = mesh.shape["row"], mesh.shape["col"]
    body = ladder_body(n_row, n_col) if (n_row, n_col) == (4, 8) else plain_body
    return jax.shard_map(body, mesh=mesh, in_specs=in_specs, out_specs=out_specs, check_vma=False)
```
